32 devices in a mesh: grp: 4 (over y, x), row: 8 (over z, core).
Axes of the slice: x: 2, y: 2, z: 4, core: 2. Of those that a mesh axis runs over, the one named last changes fastest.
Arguments:
- t_start: bfloat16 [8192, 512], P(('row', 'grp')), may hold values from -6 to 6
- h_blocks: bfloat16 [64, 4, 8, 128, 128], P('row', 'grp'), may hold values from -0.09375 to 0.09375
- h_cols: int32 [64, 4, 8], P('row', 'grp'), may hold values from 0 to 63, as said below
- t_cols: int32 [64, 3], P(('row', 'grp')), may hold values from 0 to 3, as said below
Outputs:
- t_before: bfloat16 [8192, 512], P(('row', 'grp'))
- t_last: bfloat16 [8192, 512], P(('row', 'grp'))
The draws below stay inside these ranges and needn't reach their ends.
Inputs may be any that keep to these rules, and one draw needn't show every extreme that they name: The 8 entries of h_cols[b, g] differ, and each names a block row c with (c // 2) % 4 == g. `t_cols`: the 3 entries of a row differ.
All inputs are finite; a program needn't handle non-finite values.
Results may differ from the reference program's by a relative error of at most 0.025.
Values may be sent and summed in bfloat16 or wider, within the bound.
A program may use at most 64 MiB of HBM per device.

```python
import jax
import jax.numpy as jnp
from jax import lax

BS = 128
HB = 32
STEPS = 3
RB = 2
MB = 4
TS = 3
NG = 4
HS = 8
KB = 16
NB = 64
M = 512


def draw_h_cols(key, part):
    scores = jax.random.randint(key, (NB, NG, KB), 0, 1 << 20) * KB + jnp.arange(KB, dtype=jnp.int32)
    order = jnp.argsort(scores, axis=-1)[..., :HS].astype(jnp.int32)
    group = jnp.arange(NG, dtype=jnp.int32)[None, :, None]
    return order // RB * (NG * RB) + group * RB + order % RB


def draw_t_cols(key, part):
    scores = jax.random.randint(key, (NB, MB), 0, 1 << 20) * MB + jnp.arange(MB, dtype=jnp.int32)
    return jnp.argsort(scores, axis=-1)[:, :TS].astype(jnp.int32)


def block_scale(stream_key, dims, cuts, low, largest):
    level = 1.0
    for axis_at, shards_of in cuts:
        steps = jax.random.uniform(jax.random.fold_in(jax.random.fold_in(stream_key, 6), axis_at), (shards_of,), jnp.float32, low / len(cuts), largest / len(cuts))
        level = level * jnp.repeat(jnp.exp(steps), dims[axis_at] // shards_of).reshape((-1,) + (1,) * (len(dims) - 1 - axis_at))
    return level


def scatter_about(rng, dims, deviation, reach, cuts=(), kind=jnp.bfloat16):
    array = deviation * jax.random.normal(rng, dims, jnp.float32)
    if cuts:
        array = array * block_scale(rng, dims, cuts, -0.22, 0.18)
    return jnp.clip(array, -reach, reach).astype(kind)


def setup_inputs(seed: int = 0) -> dict:
    seeds = jax.random.split(jax.random.key(seed), 5)
    return {
        "t_start": scatter_about(seeds[0], (NB * BS, M), 1.0, 6.0, ((0, 32),)),
        "h_blocks": scatter_about(seeds[1], (NB, NG, HS, BS, BS), (HB * BS) ** -0.5, 0.09375, ((0, 8), (1, 4))),
        "h_cols": draw_h_cols(jax.random.fold_in(seeds[4], 71), 0),
        "t_cols": draw_t_cols(jax.random.fold_in(seeds[4], 71), 0),
    }


def apply_hamiltonian(h_blocks, h_cols, slab):
    rows3 = slab.reshape(NB, BS, M)

    def one_row(pair):
        blocks, columns = pair
        picked = rows3[columns].astype(jnp.float32)
        partial_value = jnp.einsum("gsij,gsjm->gim", blocks.astype(jnp.float32), picked)
        rounded = lax.optimization_barrier(partial_value.astype(jnp.bfloat16))
        return jnp.sum(rounded.astype(jnp.float32), axis=0)

    return lax.map(one_row, (h_blocks, h_cols))


def reference(t_start, h_blocks, h_cols, t_cols):
    kept = jnp.any(t_cols[:, :, None] == jnp.arange(MB, dtype=jnp.int32)[None, None, :], axis=1)
    keep = kept.astype(jnp.float32)[:, None, :, None]

    def masked(values):
        shaped = values.reshape(NB, BS, MB, BS) * keep
        return shaped.reshape(NB * BS, M)

    first = masked(apply_hamiltonian(h_blocks, h_cols, t_start)).astype(jnp.bfloat16)
    before, latest = t_start, first
    for step in range(STEPS - 1):
        summed = apply_hamiltonian(h_blocks, h_cols, latest).reshape(NB * BS, M)
        after = masked(2.0 * summed - before.astype(jnp.float32)).astype(jnp.bfloat16)
        before, latest = latest, after
    return before, latest
```

```python
import functools

import jax
import jax.numpy as jnp
from jax import lax
from jax.experimental import pallas as pl
from jax.experimental.pallas import tpu as pltpu
from jax.sharding import PartitionSpec as P

BS = 128
STEPS = 3
MESH = pl.DeviceIdType.MESH
BF16 = jnp.bfloat16
F32 = jnp.float32
DENSE_BYTES = 8 << 20


def kernel(dims, t_hbm, h_hbm, hc, tc, before_ref, last_ref, *scratch):
    groups, rows, rb, cb, keeps, hrows, slots, dense = dims
    bufs = scratch[:STEPS]
    hs, hd, unp, prod, stage, landed, drow, dgrp = scratch[STEPS : STEPS + 8]
    ag_s, ag_r, fw_s, fw_r, rs_s, rs_r, dr_s, dr_r, dg_s, dg_r, local = scratch[STEPS + 8 :]
    pairs = rows // 2
    nblk = rows * rb
    g = lax.axis_index("grp")
    r = lax.axis_index("row")
    pair, core = r // 2, lax.rem(r, 2)
    sibling = pair * 2 + 1 - core
    mine = pl.ds(r * rb, rb)

    def copy(src, dst, ss, rs, row=None, grp=None):
        return pltpu.make_async_remote_copy(
            src_ref=src,
            dst_ref=dst,
            send_sem=ss,
            recv_sem=rs,
            device_id=(g if grp is None else grp, r if row is None else row),
            device_id_type=MESH,
        )

    h_copy = pltpu.make_async_copy(h_hbm.at[:, 0], hs.at[:, pl.ds(0, slots)], local.at[cb])
    h_copy.start()
    barrier = pltpu.get_barrier_semaphore()
    for k in range(1, rows):
        pl.semaphore_signal(barrier, inc=1, device_id=(g, lax.rem(r + k, rows)), device_id_type=MESH)
    for k in range(1, groups):
        pl.semaphore_signal(barrier, inc=1, device_id=(lax.rem(g + k, groups), r), device_id_type=MESH)

    t_copies = []
    for c in range(cb):
        for b in range(rb):
            one = pltpu.make_async_copy(
                t_hbm.at[pl.ds(b * BS, BS), pl.ds(c * BS, BS)],
                bufs[0].at[c, r * rb + b],
                local.at[cb + 1 + c * rb + b],
            )
            one.start()
            t_copies.append(one)
    for b in range(rb):
        total = tc[b, 0]
        for s in range(1, keeps):
            total = total + tc[b, s]
        gone = cb * (cb - 1) // 2 - total
        tile = jnp.full((16, BS), gone, jnp.int32).astype(F32).astype(BF16)
        drow[r, b] = tile
        dgrp[g, b] = tile
    for one in t_copies:
        one.wait()
    pl.semaphore_wait(barrier, rows + groups - 2)

    sends = []

    def go(one):
        one.start()
        sends.append(one)

    def gather_start(chunk, buf, c):
        own = buf.at[c, mine]
        for k in range(1, pairs):
            go(copy(own, own, ag_s.at[chunk, k], ag_r.at[chunk, k], row=lax.rem(pair + k, pairs) * 2 + core))
        go(copy(own, own, fw_s.at[chunk, 0], fw_r.at[chunk, 0], row=sibling))

    def gather_finish(chunk, buf, c):
        for k in range(1, pairs):
            src = lax.rem(pair + pairs - k, pairs)
            got = buf.at[c, pl.ds((src * 2 + core) * rb, rb)]
            copy(got, got, ag_s.at[chunk, k], ag_r.at[chunk, k], row=sibling).wait_recv()
            go(copy(got, got, fw_s.at[chunk, k], fw_r.at[chunk, k], row=sibling))
        for k in range(pairs):
            src = lax.rem(pair + pairs - k, pairs)
            got = buf.at[c, pl.ds((src * 2 + 1 - core) * rb, rb)]
            copy(got, got, fw_s.at[chunk, k], fw_r.at[chunk, k], row=sibling).wait_recv()

    for k in range(1, rows):
        go(copy(drow.at[r], drow.at[r], dr_s.at[k], dr_r.at[k], row=lax.rem(r + k, rows)))
    for k in range(1, groups):
        go(copy(dgrp.at[g], dgrp.at[g], dg_s.at[k], dg_r.at[k], grp=lax.rem(g + k, groups)))
    for c in range(cb):
        gather_start(c, bufs[0], c)

    hs[:, slots] = jnp.zeros((hrows, BS, BS), BF16)
    h_copy.wait()
    if dense:

        def build(b, carry):
            for c in range(nblk):
                named = (c // rb) * (groups * rb) + g * rb + c % rb
                at = jnp.int32(slots)
                for s in range(slots):
                    at = jnp.where(hc[b, 0, s] == named, s, at)
                hd[pl.ds(pl.multiple_of(b * BS, BS), BS), c * BS : (c + 1) * BS] = hs[b, at]
            return carry

        lax.fori_loop(0, hrows, build, 0)

    for k in range(1, rows):
        got = drow.at[lax.rem(r + rows - k, rows)]
        copy(got, got, dr_s.at[k], dr_r.at[k], row=sibling).wait_recv()
    for k in range(1, groups):
        got = dgrp.at[lax.rem(g + groups - k, groups)]
        copy(got, got, dg_s.at[k], dg_r.at[k], row=sibling).wait_recv()

    def full(tile):
        return jnp.concatenate([tile] * (BS // 16), axis=0)

    def unpacked(c, gone, packed):
        zero = jnp.zeros((BS, BS), BF16)
        if c == 0:
            value = packed(0)
        elif c == cb - 1:
            value = packed(c - 1)
        else:
            value = jnp.where(gone < c, packed(c - 1), packed(c))
        return jnp.where(gone == c, zero, value)

    def multiply(c, x):
        if dense:
            right = x[...].reshape(nblk * BS, BS)
            out = jnp.dot(hd[...], right, preferred_element_type=F32)
            prod[c] = out.astype(BF16).reshape(hrows, BS, BS)
            return

        def one_row(b, carry):
            out = jnp.zeros((BS, BS), F32)
            for s in range(slots):
                named = hc[b, 0, s]
                at = named // (groups * rb) * rb + lax.rem(named, rb)
                out = out + jnp.dot(hs[b, s], x[at], preferred_element_type=F32)
            prod[c, b] = out.astype(BF16)
            return carry

        lax.fori_loop(0, hrows, one_row, 0)

    def unpack_column(c, buf):
        def one(j, carry):
            gone = full(drow[j // rb, lax.rem(j, rb)])
            unp[c, j] = unpacked(c, gone, lambda p: buf[p, j])
            return carry

        lax.fori_loop(0, nblk, one, 0)

    def scatter_start(step, p):
        def one(i, carry):
            gone = full(dgrp[i // rb, lax.rem(i, rb)])
            stage[step, p, i] = jnp.where(gone > p, prod[p, i], prod[p + 1, i])
            return carry

        lax.fori_loop(0, hrows, one, 0)
        for k in range(1, groups):
            to = lax.rem(g + k, groups)
            go(copy(
                stage.at[step, p, pl.ds(to * rb, rb)],
                landed.at[step, p, g],
                rs_s.at[step * keeps + p, k],
                rs_r.at[step * keeps + p, k],
                grp=to,
            ))

    def scatter_finish(step, p):
        for k in range(1, groups):
            got = landed.at[step, p, lax.rem(g + groups - k, groups)]
            copy(got, got, rs_s.at[step * keeps + p, k], rs_r.at[step * keeps + p, k], row=sibling).wait_recv()
        for b in range(rb):
            gone = full(drow[r, b])
            total = stage[step, p, g * rb + b].astype(F32)
            for k in range(1, groups):
                total = total + landed[step, p, lax.rem(g + k, groups), b].astype(F32)
            at = r * rb + b
            if step == 0:
                new = total
            else:
                if step == 1:
                    old = jnp.where(gone > p, bufs[0][p, at], bufs[0][p + 1, at])
                else:
                    old = bufs[step - 1][p, at]
                new = 2.0 * total - old.astype(F32)
            new = new.astype(BF16)
            if step < STEPS - 1:
                bufs[step + 1][p, at] = new
            else:
                stage[step, p, g * rb + b] = new
        if step < STEPS - 1:
            gather_start(cb + step * keeps + p, bufs[step + 1], p)

    for step in range(STEPS):
        buf = bufs[step]
        for c in range(cb):
            if step == 0:
                gather_finish(c, buf, c)
                multiply(c, buf.at[c])
            else:
                if c < keeps:
                    gather_finish(cb + (step - 1) * keeps + c, buf, c)
                unpack_column(c, buf)
                multiply(c, unp.at[c])
            if c >= 1:
                scatter_start(step, c - 1)
            if c >= 2:
                scatter_finish(step, c - 2)
        scatter_finish(step, keeps - 1)

    for b in range(rb):
        gone = full(drow[r, b])
        for c in range(cb):
            here = (slice(b * BS, (b + 1) * BS), slice(c * BS, (c + 1) * BS))
            before_ref[here] = unpacked(c, gone, lambda p: bufs[STEPS - 1][p, r * rb + b])
            last_ref[here] = unpacked(c, gone, lambda p: stage[STEPS - 1, p, g * rb + b])
    for one in sends:
        one.wait_send()


def per_device(t_start, h_blocks, h_cols, t_cols):
    groups, rows = lax.axis_size("grp"), lax.axis_size("row")
    rb, cb = t_start.shape[0] // BS, t_start.shape[1] // BS
    hrows, slots = h_blocks.shape[0], h_blocks.shape[2]
    keeps = t_cols.shape[1]
    nblk = rows * rb
    pairs = rows // 2
    dense = hrows * nblk * BS * BS * 2 <= DENSE_BYTES
    chunks = cb + (STEPS - 1) * keeps
    dma = pltpu.SemaphoreType.DMA
    out = jax.ShapeDtypeStruct(t_start.shape, t_start.dtype)
    return pl.pallas_call(
        functools.partial(kernel, (groups, rows, rb, cb, keeps, hrows, slots, dense)),
        out_shape=(out, out),
        in_specs=[
            pl.BlockSpec(memory_space=pl.ANY),
            pl.BlockSpec(memory_space=pl.ANY),
            pl.BlockSpec(memory_space=pltpu.SMEM),
            pl.BlockSpec(memory_space=pltpu.SMEM),
        ],
        out_specs=(pl.BlockSpec(memory_space=pltpu.VMEM),) * 2,
        scratch_shapes=[
            pltpu.VMEM((cb, nblk, BS, BS), BF16),
            *[pltpu.VMEM((keeps, nblk, BS, BS), BF16) for _ in range(STEPS - 1)],
            pltpu.VMEM((hrows, slots + 1, BS, BS), BF16),
            pltpu.VMEM((hrows * BS, nblk * BS) if dense else (16, BS), BF16),
            pltpu.VMEM((cb, nblk, BS, BS), BF16),
            pltpu.VMEM((cb, hrows, BS, BS), BF16),
            pltpu.VMEM((STEPS, keeps, hrows, BS, BS), BF16),
            pltpu.VMEM((STEPS, keeps, groups, rb, BS, BS), BF16),
            pltpu.VMEM((rows, rb, 16, BS), BF16),
            pltpu.VMEM((groups, rb, 16, BS), BF16),
            dma((chunks, pairs)),
            dma((chunks, pairs)),
            dma((chunks, pairs)),
            dma((chunks, pairs)),
            dma((STEPS * keeps, groups)),
            dma((STEPS * keeps, groups)),
            dma((rows,)),
            dma((rows,)),
            dma((groups,)),
            dma((groups,)),
            dma((cb + 1 + cb * rb,)),
        ],
        compiler_params=pltpu.CompilerParams(
            collective_id=0, has_side_effects=True, vmem_limit_bytes=56 << 20
        ),
    )(t_start, h_blocks, h_cols, t_cols)


def solution(mesh):
    placed = (
        P(("row", "grp"), None),
        P("row", "grp", None, None, None),
        P("row", "grp", None),
        P(("row", "grp"), None),
    )
    return jax.shard_map(
        per_device,
        mesh=mesh,
        in_specs=placed,
        out_specs=(P(("row", "grp"), None), P(("row", "grp"), None)),
        check_vma=False,
    )
```

```python
import functools

import jax
import jax.numpy as jnp
from jax import lax
from jax.experimental import pallas as pl
from jax.experimental.pallas import tpu as pltpu
from jax.sharding import PartitionSpec as P

BS = 128
STEPS = 3
MESH = pl.DeviceIdType.MESH
BF16 = jnp.bfloat16
F32 = jnp.float32
DENSE_BYTES = 8 << 20


def kernel(dims, t_hbm, h_hbm, hc, tc, before_ref, last_ref, *scratch):
    groups, rows, rb, cb, keeps, hrows, slots, dense = dims
    bufs = scratch[:STEPS]
    hs, hd, unp, prod, stage, landed, drow, dgrp = scratch[STEPS : STEPS + 8]
    ag_s, ag_r, fw_s, fw_r, rs_s, rs_r, dr_s, dr_r, dg_s, dg_r, local = scratch[STEPS + 8 :]
    pairs = rows // 2
    nblk = rows * rb
    g = lax.axis_index("grp")
    r = lax.axis_index("row")
    pair, core = r // 2, lax.rem(r, 2)
    sibling = pair * 2 + 1 - core
    mine = pl.ds(r * rb, rb)

    def copy(src, dst, ss, rs, row=None, grp=None):
        return pltpu.make_async_remote_copy(
            src_ref=src,
            dst_ref=dst,
            send_sem=ss,
            recv_sem=rs,
            device_id=(g if grp is None else grp, r if row is None else row),
            device_id_type=MESH,
        )

    h_copy = pltpu.make_async_copy(h_hbm.at[:, 0], hs.at[:, pl.ds(0, slots)], local.at[cb])
    h_copy.start()
    barrier = pltpu.get_barrier_semaphore()
    for k in range(1, rows):
        pl.semaphore_signal(barrier, inc=1, device_id=(g, lax.rem(r + k, rows)), device_id_type=MESH)
    for k in range(1, groups):
        pl.semaphore_signal(barrier, inc=1, device_id=(lax.rem(g + k, groups), r), device_id_type=MESH)

    t_copies = []
    for c in range(cb):
        for b in range(rb):
            one = pltpu.make_async_copy(
                t_hbm.at[pl.ds(b * BS, BS), pl.ds(c * BS, BS)],
                bufs[0].at[c, r * rb + b],
                local.at[cb + 1 + c * rb + b],
            )
            one.start()
            t_copies.append(one)
    for b in range(rb):
        total = tc[b, 0]
        for s in range(1, keeps):
            total = total + tc[b, s]
        gone = cb * (cb - 1) // 2 - total
        tile = jnp.full((16, BS), gone, jnp.int32).astype(F32).astype(BF16)
        drow[r, b] = tile
        dgrp[g, b] = tile
    for one in t_copies:
        one.wait()
    pl.semaphore_wait(barrier, rows + groups - 2)

    sends = []

    def go(one):
        one.start()
        sends.append(one)

    def gather_start(chunk, buf, c):
        own = buf.at[c, mine]
        for k in range(1, pairs):
            go(copy(own, own, ag_s.at[chunk, k], ag_r.at[chunk, k], row=lax.rem(pair + k, pairs) * 2 + core))
        go(copy(own, own, fw_s.at[chunk, 0], fw_r.at[chunk, 0], row=sibling))

    def gather_finish(chunk, buf, c):
        for k in range(1, pairs):
            src = lax.rem(pair + pairs - k, pairs)
            got = buf.at[c, pl.ds((src * 2 + core) * rb, rb)]
            copy(got, got, ag_s.at[chunk, k], ag_r.at[chunk, k], row=sibling).wait_recv()
            go(copy(got, got, fw_s.at[chunk, k], fw_r.at[chunk, k], row=sibling))
        for k in range(pairs):
            src = lax.rem(pair + pairs - k, pairs)
            got = buf.at[c, pl.ds((src * 2 + 1 - core) * rb, rb)]
            copy(got, got, fw_s.at[chunk, k], fw_r.at[chunk, k], row=sibling).wait_recv()

    for k in range(1, rows):
        go(copy(drow.at[r], drow.at[r], dr_s.at[k], dr_r.at[k], row=lax.rem(r + k, rows)))
    for k in range(1, groups):
        go(copy(dgrp.at[g], dgrp.at[g], dg_s.at[k], dg_r.at[k], grp=lax.rem(g + k, groups)))
    for c in range(2):
        gather_start(c, bufs[0], c)

    hs[:, slots] = jnp.zeros((hrows, BS, BS), BF16)
    h_copy.wait()
    if dense:

        def build(b, carry):
            for c in range(nblk):
                named = (c // rb) * (groups * rb) + g * rb + c % rb
                at = jnp.int32(slots)
                for s in range(slots):
                    at = jnp.where(hc[b, 0, s] == named, s, at)
                hd[pl.ds(pl.multiple_of(b * BS, BS), BS), c * BS : (c + 1) * BS] = hs[b, at]
            return carry

        lax.fori_loop(0, hrows, build, 0)

    def full(tile):
        return jnp.concatenate([tile] * (BS // 16), axis=0)

    def unpacked(c, gone, packed):
        zero = jnp.zeros((BS, BS), BF16)
        if c == 0:
            value = packed(0)
        elif c == cb - 1:
            value = packed(c - 1)
        else:
            value = jnp.where(gone < c, packed(c - 1), packed(c))
        return jnp.where(gone == c, zero, value)

    def multiply(c, x):
        if dense:
            right = x[...].reshape(nblk * BS, BS)
            out = jnp.dot(hd[...], right, preferred_element_type=F32)
            prod[c] = out.astype(BF16).reshape(hrows, BS, BS)
            return

        def one_row(b, carry):
            out = jnp.zeros((BS, BS), F32)
            for s in range(slots):
                named = hc[b, 0, s]
                at = named // (groups * rb) * rb + lax.rem(named, rb)
                out = out + jnp.dot(hs[b, s], x[at], preferred_element_type=F32)
            prod[c, b] = out.astype(BF16)
            return carry

        lax.fori_loop(0, hrows, one_row, 0)

    def unpack_column(c, buf):
        def one(j, carry):
            gone = full(drow[j // rb, lax.rem(j, rb)])
            unp[c, j] = unpacked(c, gone, lambda p: buf[p, j])
            return carry

        lax.fori_loop(0, nblk, one, 0)

    def scatter_start(step, p):
        def one(i, carry):
            gone = full(dgrp[i // rb, lax.rem(i, rb)])
            stage[step, p, i] = jnp.where(gone > p, prod[p, i], prod[p + 1, i])
            return carry

        lax.fori_loop(0, hrows, one, 0)
        for k in range(1, groups):
            to = lax.rem(g + k, groups)
            go(copy(
                stage.at[step, p, pl.ds(to * rb, rb)],
                landed.at[step, p, g],
                rs_s.at[step * keeps + p, k],
                rs_r.at[step * keeps + p, k],
                grp=to,
            ))

    def scatter_finish(step, p):
        for k in range(1, groups):
            got = landed.at[step, p, lax.rem(g + groups - k, groups)]
            copy(got, got, rs_s.at[step * keeps + p, k], rs_r.at[step * keeps + p, k], row=sibling).wait_recv()
        for b in range(rb):
            gone = full(drow[r, b])
            total = stage[step, p, g * rb + b].astype(F32)
            for k in range(1, groups):
                total = total + landed[step, p, lax.rem(g + k, groups), b].astype(F32)
            at = r * rb + b
            if step == 0:
                new = total
            else:
                if step == 1:
                    old = jnp.where(gone > p, bufs[0][p, at], bufs[0][p + 1, at])
                else:
                    old = bufs[step - 1][p, at]
                new = 2.0 * total - old.astype(F32)
            new = new.astype(BF16)
            if step < STEPS - 1:
                bufs[step + 1][p, at] = new
            else:
                stage[step, p, g * rb + b] = new
        if step < STEPS - 1:
            gather_start(cb + step * keeps + p, bufs[step + 1], p)

    for step in range(STEPS):
        buf = bufs[step]
        for c in range(cb):
            if step == 0:
                gather_finish(c, buf, c)
                if c + 2 < cb:
                    gather_start(c + 2, buf, c + 2)
                multiply(c, buf.at[c])
            else:
                if c < keeps:
                    gather_finish(cb + (step - 1) * keeps + c, buf, c)
                unpack_column(c, buf)
                multiply(c, unp.at[c])
            if step == 0 and c == 1:
                for k in range(1, rows):
                    got = drow.at[lax.rem(r + rows - k, rows)]
                    copy(got, got, dr_s.at[k], dr_r.at[k], row=sibling).wait_recv()
                for k in range(1, groups):
                    got = dgrp.at[lax.rem(g + groups - k, groups)]
                    copy(got, got, dg_s.at[k], dg_r.at[k], row=sibling).wait_recv()
            if c >= 1:
                scatter_start(step, c - 1)
            if c >= 2:
                scatter_finish(step, c - 2)
        scatter_finish(step, keeps - 1)

    for b in range(rb):
        gone = full(drow[r, b])
        for c in range(cb):
            here = (slice(b * BS, (b + 1) * BS), slice(c * BS, (c + 1) * BS))
            before_ref[here] = unpacked(c, gone, lambda p: bufs[STEPS - 1][p, r * rb + b])
            last_ref[here] = unpacked(c, gone, lambda p: stage[STEPS - 1, p, g * rb + b])
    for one in sends:
        one.wait_send()


def per_device(t_start, h_blocks, h_cols, t_cols):
    groups, rows = lax.axis_size("grp"), lax.axis_size("row")
    rb, cb = t_start.shape[0] // BS, t_start.shape[1] // BS
    hrows, slots = h_blocks.shape[0], h_blocks.shape[2]
    keeps = t_cols.shape[1]
    nblk = rows * rb
    pairs = rows // 2
    dense = hrows * nblk * BS * BS * 2 <= DENSE_BYTES
    chunks = cb + (STEPS - 1) * keeps
    dma = pltpu.SemaphoreType.DMA
    out = jax.ShapeDtypeStruct(t_start.shape, t_start.dtype)
    return pl.pallas_call(
        functools.partial(kernel, (groups, rows, rb, cb, keeps, hrows, slots, dense)),
        out_shape=(out, out),
        in_specs=[
            pl.BlockSpec(memory_space=pl.ANY),
            pl.BlockSpec(memory_space=pl.ANY),
            pl.BlockSpec(memory_space=pltpu.SMEM),
            pl.BlockSpec(memory_space=pltpu.SMEM),
        ],
        out_specs=(pl.BlockSpec(memory_space=pltpu.VMEM),) * 2,
        scratch_shapes=[
            pltpu.VMEM((cb, nblk, BS, BS), BF16),
            *[pltpu.VMEM((keeps, nblk, BS, BS), BF16) for _ in range(STEPS - 1)],
            pltpu.VMEM((hrows, slots + 1, BS, BS), BF16),
            pltpu.VMEM((hrows * BS, nblk * BS) if dense else (16, BS), BF16),
            pltpu.VMEM((cb, nblk, BS, BS), BF16),
            pltpu.VMEM((cb, hrows, BS, BS), BF16),
            pltpu.VMEM((STEPS, keeps, hrows, BS, BS), BF16),
            pltpu.VMEM((STEPS, keeps, groups, rb, BS, BS), BF16),
            pltpu.VMEM((rows, rb, 16, BS), BF16),
            pltpu.VMEM((groups, rb, 16, BS), BF16),
            dma((chunks, pairs)),
            dma((chunks, pairs)),
            dma((chunks, pairs)),
            dma((chunks, pairs)),
            dma((STEPS * keeps, groups)),
            dma((STEPS * keeps, groups)),
            dma((rows,)),
            dma((rows,)),
            dma((groups,)),
            dma((groups,)),
            dma((cb + 1 + cb * rb,)),
        ],
        compiler_params=pltpu.CompilerParams(
            collective_id=0, has_side_effects=True, vmem_limit_bytes=56 << 20
        ),
    )(t_start, h_blocks, h_cols, t_cols)


def solution(mesh):
    placed = (
        P(("row", "grp"), None),
        P("row", "grp", None, None, None),
        P("row", "grp", None),
        P(("row", "grp"), None),
    )
    return jax.shard_map(
        per_device,
        mesh=mesh,
        in_specs=placed,
        out_specs=(P(("row", "grp"), None), P(("row", "grp"), None)),
        check_vma=False,
    )
```
